32 devices in a mesh: dom: 16 (over z, x, core), band: 2 (over y).
Axes of the slice: x: 2, y: 2, z: 4, core: 2. Of those that a mesh axis runs over, the one named last changes fastest.
Arguments:
- ensemble: float32 [16, 3, 32, 4096], P('dom', None, 'band'), may hold values from -6 to 6
- ancestors: int32 [16], P('dom'), may hold values from 0 to 15
- sea_depth: float32 [32, 4096], P('band'), may hold values from 1 to 2
- obs_rows: int32 [4096], P('band'), may hold values from 0 to 31, as said below
- obs_cols: int32 [4096], P('band'), may hold values from 0 to 4095
- obs_values: float32 [4096], P('band'), may hold values from -6 to 6
Outputs:
- forecast: float32 [16, 3, 32, 4096], P('dom', None, 'band')
The draws below stay inside these ranges and needn't reach their ends.
Inputs may be any that keep to these rules, and one draw needn't show every extreme that they name: `obs_rows`: observations b * 2048 to (b + 1) * 2048 - 1 lie in rows b * 16 to (b + 1) * 16 - 1; no two observations share a cell.
All inputs are finite; a program needn't handle non-finite values.
Results may differ from the reference program's by a relative error of at most 0.00016.
Values sent between devices are 32-bit elements; how exact they have to be, the bound alone decides.
A program may use at most 64 MiB of HBM per device.

```python
import math
import jax
import jax.numpy as jnp
import numpy as np
from jax import lax

ROWS_DEV = 16
NCOL = 4096
OBS_BAND = 2048
STEPS = 4
BW = 8
PARTICLES = 16
NROWS = 32
NOBS = 4096


def obs_cells(key):
    band_count = NROWS // ROWS_DEV
    band_keys = jax.random.split(jax.random.fold_in(key, 7), band_count)

    def one_band(band_key):
        return jax.random.permutation(band_key, ROWS_DEV * NCOL)[:OBS_BAND]
    cells = jax.vmap(one_band)(band_keys)
    offsets = (jnp.arange(band_count) * ROWS_DEV)[:, None]
    row_part = (cells // NCOL + offsets).reshape(-1).astype(jnp.int32)
    col_part = (cells % NCOL).reshape(-1).astype(jnp.int32)
    return (row_part, col_part)


def draw_obs_rows(key, part):
    return obs_cells(key)[0]


def draw_obs_cols(key, part):
    return obs_cells(key)[1]


def touch_ends(values, own_key, least, largest):
    longest = values.shape.index(max(values.shape))
    spots = []
    for shift in (0, 1):
        where = [jax.random.randint(jax.random.fold_in(own_key, axis), (), 0, length) for axis, length in enumerate(values.shape)]
        where[longest] = (where[longest] + shift) % values.shape[longest]
        spots.append(tuple(where))
    return values.at[spots[0]].set(least).at[spots[1]].set(largest)


def shard_levels(stream_key, extent, cuts, low, top_value):
    def one(position, shards_of):
        steps = jax.random.uniform(jax.random.fold_in(jax.random.fold_in(stream_key, 6), position), (shards_of,), jnp.float32, low / len(cuts), top_value / len(cuts))
        return jnp.repeat(jnp.exp(steps), extent[position] // shards_of).reshape((-1,) + (1,) * (len(extent) - position - 1))

    level = one(*cuts[0])
    for cut in cuts[1:]:
        level = level * one(*cut)
    return level


def rank_table(count, skew):
    weights = [(1 << 20) // math.isqrt(grade ** skew) + 1 for grade in range(1, count + 1)]
    width = 1 + sum(weights) // (1 << 30)
    return np.cumsum(np.array([max(1, weight // width) for weight in weights]))


def skewed_ids(stream_key, shape, count, slope):
    listing = rank_table(count, slope)
    ticket = jax.random.randint(jax.random.fold_in(stream_key, 1), shape, 0, int(listing[count - 1]))
    rank = jnp.searchsorted(jnp.asarray(listing, jnp.int32), ticket, side="right")
    return jax.random.permutation(jax.random.fold_in(stream_key, 2), count)[rank].astype(jnp.int32)


def normal_values(key, dims, width, reach, cuts=(), kind=jnp.bfloat16):
    level = shard_levels(key, dims, cuts, -0.22, 0.18) if cuts else 1.0
    entries = jax.random.normal(key, dims, jnp.float32) * width * level
    return jnp.minimum(jnp.maximum(entries, -reach), reach).astype(kind)


def setup_inputs(seed: int = 0) -> dict:
    key_of = jax.random.split(jax.random.key(seed), 7)
    return {
        "ensemble": normal_values(key_of[0], (PARTICLES, 3, NROWS, NCOL), 1.0, 6.0, ((0, 16), (2, 2)), jnp.float32),
        "ancestors": touch_ends(skewed_ids(key_of[1], (PARTICLES,), PARTICLES, 2), jax.random.fold_in(key_of[1], 3), 0, PARTICLES - 1).astype(jnp.int32),
        "sea_depth": jnp.clip(jnp.exp(math.log(2.0) - 0.6931472 * jax.random.uniform(key_of[2], (NROWS, NCOL), jnp.float32) ** shard_levels(key_of[2], (NROWS, NCOL), ((0, 2),), -0.2, 0.2)), 1.0, 2.0),
        "obs_rows": draw_obs_rows(jax.random.fold_in(key_of[6], 71), 0),
        "obs_cols": draw_obs_cols(jax.random.fold_in(key_of[6], 71), 0),
        "obs_values": normal_values(key_of[5], (NOBS,), 1.0, 6.0, ((0, 2),), jnp.float32),
    }


TIME_STEP = 0.8
NUDGE_GAIN = 0.5
LENGTH_SCALE = 3.0


def kernel_weight(offset):
    return jnp.exp(jnp.float32(-abs(offset) / LENGTH_SCALE))


def band_smooth(field, axis_no):
    count = field.shape[axis_no]
    widths = [(0, 0), (0, 0)]
    widths[axis_no] = (BW, BW)
    padded = jnp.pad(field, widths)
    total = jnp.zeros_like(field)
    for offset in range(-BW, BW + 1):
        piece = lax.slice_in_dim(padded, BW + offset, BW + offset + count, axis=axis_no)
        total = total + kernel_weight(offset) * piece
    return total


def advance(height, east_vel, north_vel, sea_depth, coriolis):
    flux_east = sea_depth * east_vel
    flux_north = jnp.pad(sea_depth * north_vel, ((1, 1), (0, 0)))
    east_diff = 0.5 * (jnp.roll(flux_east, -1, -1) - jnp.roll(flux_east, 1, -1))
    north_diff = 0.5 * (flux_north[2:] - flux_north[:-2])
    new_height = height - TIME_STEP * (east_diff + north_diff)
    padded = jnp.pad(new_height, ((1, 1), (0, 0)))
    slope_east = 0.5 * (jnp.roll(new_height, -1, -1) - jnp.roll(new_height, 1, -1))
    slope_north = 0.5 * (padded[2:] - padded[:-2])
    new_east = east_vel + TIME_STEP * (coriolis * north_vel - slope_east)
    new_north = north_vel + TIME_STEP * (-coriolis * east_vel - slope_north)
    return new_height, new_east, new_north


def reference(ensemble, ancestors, sea_depth, obs_rows, obs_cols, obs_values):
    children = ensemble[ancestors]
    row_index = jnp.arange(NROWS)
    coriolis = (0.1 + 0.4 * ((row_index.astype(jnp.float32) + 0.5) / NROWS))[:, None]

    def evolve_one(particle):
        height, east_vel, north_vel = particle[0], particle[1], particle[2]
        innovation = obs_values - height[obs_rows, obs_cols]
        scattered = jnp.zeros((NROWS, NCOL), jnp.float32).at[obs_rows, obs_cols].add(innovation)
        spread = band_smooth(scattered, 1)
        increment = band_smooth(spread, 0)
        height = height + NUDGE_GAIN * increment
        for section_no in range(STEPS):
            height, east_vel, north_vel = advance(height, east_vel, north_vel, sea_depth, coriolis)
        return jnp.stack([height, east_vel, north_vel])

    return lax.map(evolve_one, children)
```

```python
import functools
import math

import jax
import jax.numpy as jnp
from jax import lax
from jax.experimental import pallas as pl
from jax.experimental.pallas import tpu as pltpu
from jax.sharding import PartitionSpec as P

STEPS = 4
BW = 8
TIME_STEP = 0.8
NUDGE_GAIN = 0.5
LENGTH_SCALE = 3.0
LANES = 128
MARGIN = 2 * STEPS


def weight(offset):
    distance = jnp.abs(offset).astype(jnp.float32)
    return jnp.where(distance <= BW, jnp.exp(-distance / LENGTH_SCALE), jnp.float32(0.0))


def cycle(
    doms, bands, rows, cols, win,
    ens, anc, depth, pos, val, out,
    hb, hw, uw, vw, dw, posb, valb, field, spread, done, relay, chosen, lineage,
    band_send, band_recv, anc_send, anc_recv, s1_send, s1_recv, s2_send, s2_recv, own_sem,
):
    me = lax.axis_index("dom")
    band = lax.axis_index("band")
    chunk = cols // doms
    blocks = cols // LANES
    wide = rows + 2 * MARGIN
    body = pl.ds(LANES, cols)

    barrier = pltpu.get_barrier_semaphore()
    for k in range(1, doms):
        pl.semaphore_signal(barrier, inc=1, device_id={"dom": lax.rem(me + k, doms)})

    has_up = band > 0
    has_down = band < bands - 1

    @pl.when(has_up)
    def _():
        pl.semaphore_signal(barrier, inc=1, device_id={"band": band - 1})

    @pl.when(has_down)
    def _():
        pl.semaphore_signal(barrier, inc=1, device_id={"band": band + 1})

    neighbours = jnp.minimum(band, 1) + jnp.minimum(bands - 1 - band, 1)
    pl.semaphore_wait(barrier, doms - 1 + neighbours)

    def band_copies(up, first=0, last=6):
        edge = pl.ds(0, MARGIN) if up else pl.ds(rows - MARGIN, MARGIN)
        halo = pl.ds(MARGIN + rows, MARGIN) if up else pl.ds(0, MARGIN)
        slot = 2 if up else 0
        way = 0 if up else 1
        target = {"band": band - 1} if up else {"band": band + 1}
        pairs = [
            (pos, posb.at[slot]),
            (val, valb.at[slot]),
            (ens.at[0, 0], hb.at[pl.ds(slot * rows, rows)]),
            (ens.at[0, 1, edge], uw.at[halo, body]),
            (ens.at[0, 2, edge], vw.at[halo, body]),
            (depth.at[edge], dw.at[halo, body]),
        ]
        return [
            pltpu.make_async_remote_copy(
                src_ref=src, dst_ref=dst,
                send_sem=band_send.at[way, i], recv_sem=band_recv.at[way, i],
                device_id=target,
            )
            for i, (src, dst) in list(enumerate(pairs))[first:last]
        ]

    @pl.when(has_up)
    def _():
        for copy in band_copies(True):
            copy.start()

    @pl.when(has_down)
    def _():
        for copy in band_copies(False):
            copy.start()

    def anc_copy(k):
        return pltpu.make_async_remote_copy(
            src_ref=anc, dst_ref=lineage.at[me],
            send_sem=anc_send.at[k], recv_sem=anc_recv.at[k],
            device_id={"dom": lax.rem(me + k, doms)},
        )

    for k in range(1, doms):
        anc_copy(k).start()
    lineage[me] = anc[...]

    own = pl.ds(MARGIN, rows)
    hb[rows : 2 * rows] = ens[0, 0]
    uw[own, body] = ens[0, 1]
    vw[own, body] = ens[0, 2]
    dw[own, body] = depth[...]
    field[0] = jnp.zeros((3 * rows, LANES), jnp.float32)
    field[blocks + 1] = jnp.zeros((3 * rows, LANES), jnp.float32)

    def place(slot, where_ref, value_ref):
        where, value = where_ref[...], value_ref[...]
        count = where.shape[1]
        group = where >> 7
        lane = where & (LANES - 1)
        high = value.astype(jnp.bfloat16).astype(jnp.float32)
        low = value - high
        hit = lax.broadcasted_iota(jnp.int32, (LANES, count), 0) == lane
        right = jnp.concatenate(
            [
                jnp.where(hit, high, 0.0).astype(jnp.bfloat16),
                jnp.where(hit, low, 0.0).astype(jnp.bfloat16),
                jnp.where(hit, 1.0, 0.0).astype(jnp.bfloat16),
            ],
            axis=0,
        )
        per = 8
        for first in range(0, blocks, per):
            index = lax.broadcasted_iota(jnp.int32, (per * rows, count), 0) + first * rows
            left = jnp.where(index == group, 1.0, 0.0).astype(jnp.bfloat16)
            placed = lax.dot_general(
                left, right, (((1,), (1,)), ((), ())), preferred_element_type=jnp.float32
            )
            for j in range(per):
                part = placed[j * rows : (j + 1) * rows]
                height = hb[slot * rows : (slot + 1) * rows, (first + j) * LANES : (first + j + 1) * LANES]
                field[first + j + 1, slot * rows : (slot + 1) * rows, :] = (
                    part[:, :LANES] + part[:, LANES : 2 * LANES] - part[:, 2 * LANES :] * height
                )

    place(1, pos, val)

    def blank(slot):
        field[:, slot * rows : (slot + 1) * rows, :] = jnp.zeros(
            (blocks + 2, rows, LANES), jnp.float32
        )
        halo = pl.ds(0, MARGIN) if slot == 0 else pl.ds(MARGIN + rows, MARGIN)
        hb[slot * rows : (slot + 1) * rows] = jnp.zeros((rows, cols), jnp.float32)
        for ref in (uw, vw, dw):
            ref[halo, body] = jnp.zeros((MARGIN, cols), jnp.float32)

    @pl.when(has_up)
    def _():
        for copy in band_copies(False, 0, 3):
            copy.wait_recv()
        place(0, posb.at[0], valb.at[0])

    @pl.when(jnp.logical_not(has_up))
    def _():
        blank(0)

    @pl.when(has_down)
    def _():
        for copy in band_copies(True, 0, 3):
            copy.wait_recv()
        place(2, posb.at[2], valb.at[2])

    @pl.when(jnp.logical_not(has_down))
    def _():
        blank(2)

    apart = lax.broadcasted_iota(jnp.int32, (LANES, LANES), 1) - lax.broadcasted_iota(
        jnp.int32, (LANES, LANES), 0
    )
    mats = [weight(apart + LANES), weight(apart), weight(apart - LANES)]
    global_row = band * rows - MARGIN + lax.broadcasted_iota(jnp.int32, (wide, 1), 0)
    inside = (global_row >= 0) & (global_row < bands * rows)
    per = 8
    for first in range(0, blocks, per):
        total = None
        for i in range(3):
            part = field[first + i : first + i + per].reshape(per * 3 * rows, LANES)
            term = jnp.dot(
                part, mats[i], precision=lax.Precision.HIGHEST, preferred_element_type=jnp.float32
            )
            total = term if total is None else total + term
        spread[first : first + per] = total.reshape(per, 3 * rows, LANES)
    base = rows - MARGIN
    for j in range(blocks):
        increment = None
        for offset in range(2 * BW + 1):
            factor = math.exp(-abs(offset - BW) / LENGTH_SCALE)
            first = base - BW + offset
            term = factor * spread[j, first : first + wide, :]
            increment = term if increment is None else increment + term
        columns = pl.ds(j * LANES, LANES)
        hw[:, (j + 1) * LANES : (j + 2) * LANES] = jnp.where(
            inside, hb[base : base + wide, columns] + NUDGE_GAIN * increment, 0.0
        )

    @pl.when(has_up)
    def _():
        for copy in band_copies(False, 3, 6):
            copy.wait_recv()

    @pl.when(has_down)
    def _():
        for copy in band_copies(True, 3, 6):
            copy.wait_recv()

    for ref in (hw, uw, vw, dw):
        ref[:, 0:LANES] = ref[:, cols : cols + LANES]
        ref[:, cols + LANES : cols + 2 * LANES] = ref[:, LANES : 2 * LANES]

    turning = 0.1 + 0.4 * ((global_row.astype(jnp.float32) + 0.5) / (bands * rows))
    turn = TIME_STEP * turning
    span = win + 2 * LANES
    windows = cols // win
    each = win // chunk

    def after(x, axis):
        return pltpu.roll(x, x.shape[axis] - 1, axis)

    def before(x, axis):
        return pltpu.roll(x, 1, axis)

    def s1_copy(k, target):
        return pltpu.make_async_remote_copy(
            src_ref=done.at[:, :, pl.ds(pl.multiple_of(target * chunk, LANES), chunk)],
            dst_ref=relay.at[me],
            send_sem=s1_send.at[k], recv_sem=s1_recv.at[k],
            device_id={"dom": target},
        )

    def window(step, carry):
        w = lax.rem(step + me, windows)
        at = pl.ds(pl.multiple_of(w * win, LANES), span)
        h, u, v, d = hw[:, at], uw[:, at], vw[:, at], dw[:, at]
        half = 0.5 * TIME_STEP
        for _ in range(STEPS):
            east, north = d * u, d * v
            diff = (after(east, 1) - before(east, 1)) + (after(north, 0) - before(north, 0))
            h = jnp.where(inside, h - half * diff, 0.0)
            new_u = u + (turn * v - half * (after(h, 1) - before(h, 1)))
            new_v = v - (turn * u + half * (after(h, 0) - before(h, 0)))
            u = jnp.where(inside, new_u, 0.0)
            v = jnp.where(inside, new_v, 0.0)
        target_cols = pl.ds(pl.multiple_of(w * win, LANES), win)
        for i, x in enumerate((h, u, v)):
            done[i, :, target_cols] = x[MARGIN : MARGIN + rows, LANES : LANES + win]
        for i in range(each):
            target = w * each + i

            @pl.when(target != me)
            def _():
                s1_copy(lax.rem(target - me + doms, doms), target).start()

        return carry

    lax.fori_loop(0, windows, window, 0)
    relay[me] = done[:, :, pl.ds(pl.multiple_of(me * chunk, LANES), chunk)]

    for k in range(1, doms):
        anc_copy(k).wait_recv()
        s1_copy(k, lax.rem(me + k, doms)).wait_recv()

    def s2_copy(k):
        target = lax.rem(me + k, doms)
        return pltpu.make_async_remote_copy(
            src_ref=chosen.at[target],
            dst_ref=out.at[0, :, :, pl.ds(pl.multiple_of(me * chunk, LANES), chunk)],
            send_sem=s2_send.at[k], recv_sem=s2_recv.at[k],
            device_id={"dom": target},
        )

    def pick(child):
        parent = lineage[child][0:1, 0:1]
        for i in range(3):
            best = relay[0, i]
            for p in range(1, doms):
                best = jnp.where(parent == p, relay[p, i], best)
            chosen[child, i] = best

    def send(k, carry):
        pick(lax.rem(me + k, doms))
        s2_copy(k).start()
        return carry

    lax.fori_loop(1, doms, send, 0)
    pick(me)
    own_copy = pltpu.make_async_copy(
        chosen.at[me],
        out.at[0, :, :, pl.ds(pl.multiple_of(me * chunk, LANES), chunk)],
        own_sem,
    )
    own_copy.start()

    @pl.when(has_up)
    def _():
        for copy in band_copies(True):
            copy.wait_send()

    @pl.when(has_down)
    def _():
        for copy in band_copies(False):
            copy.wait_send()

    for k in range(1, doms):
        anc_copy(k).wait_send()
        s1_copy(k, lax.rem(me + k, doms)).wait_send()
    own_copy.wait()
    for k in range(1, doms):
        s2_copy(k).wait()


def on_device(doms, bands, ensemble, ancestors, sea_depth, obs_rows, obs_cols, obs_values):
    _, fields, rows, cols = ensemble.shape
    count = obs_rows.shape[0]
    local_rows = obs_rows - lax.axis_index("band") * rows
    pos = (((obs_cols >> 7) * rows + local_rows) * LANES + (obs_cols & (LANES - 1)))[None, :]
    anc = jnp.broadcast_to(ancestors[:, None], (8, LANES))
    chunk = cols // doms
    blocks = cols // LANES
    win = 1024
    wide = rows + 2 * MARGIN
    f32 = jnp.float32
    dma = pltpu.SemaphoreType.DMA
    vmem = pl.BlockSpec(memory_space=pltpu.VMEM)
    return pl.pallas_call(
        functools.partial(cycle, doms, bands, rows, cols, win),
        out_shape=jax.ShapeDtypeStruct(ensemble.shape, f32),
        in_specs=[vmem] * 5,
        out_specs=pl.BlockSpec(memory_space=pl.ANY),
        scratch_shapes=[
            pltpu.VMEM((3 * rows, cols), f32),
            pltpu.VMEM((wide, cols + 2 * LANES), f32),
            pltpu.VMEM((wide, cols + 2 * LANES), f32),
            pltpu.VMEM((wide, cols + 2 * LANES), f32),
            pltpu.VMEM((wide, cols + 2 * LANES), f32),
            pltpu.VMEM((3, 1, count), jnp.int32),
            pltpu.VMEM((3, 1, count), f32),
            pltpu.VMEM((blocks + 2, 3 * rows, LANES), f32),
            pltpu.VMEM((blocks, 3 * rows, LANES), f32),
            pltpu.VMEM((fields, rows, cols), f32),
            pltpu.VMEM((doms, fields, rows, chunk), f32),
            pltpu.VMEM((doms, fields, rows, chunk), f32),
            pltpu.VMEM((doms, 8, LANES), jnp.int32),
            dma((2, 6)),
            dma((2, 6)),
            dma((doms,)),
            dma((doms,)),
            dma((doms,)),
            dma((doms,)),
            dma((doms,)),
            dma((doms,)),
            dma,
        ],
        compiler_params=pltpu.CompilerParams(
            collective_id=0, has_side_effects=True, vmem_limit_bytes=48 * 1024 * 1024
        ),
        name="cycle",
    )(ensemble, anc, sea_depth, pos, obs_values[None, :])


def solution(mesh):
    placed = (
        P("dom", None, "band", None),
        P("dom"),
        P("band", None),
        P("band"),
        P("band"),
        P("band"),
    )
    return jax.shard_map(
        functools.partial(on_device, mesh.shape["dom"], mesh.shape["band"]),
        mesh=mesh,
        in_specs=placed,
        out_specs=P("dom", None, "band", None),
        check_vma=False,
    )
```

```python
import functools
import math

import jax
import jax.numpy as jnp
from jax import lax
from jax.experimental import pallas as pl
from jax.experimental.pallas import tpu as pltpu
from jax.sharding import PartitionSpec as P

STEPS = 4
BW = 8
TIME_STEP = 0.8
NUDGE_GAIN = 0.5
LENGTH_SCALE = 3.0
LANES = 128
MARGIN = 2 * STEPS


def weight(offset):
    distance = jnp.abs(offset).astype(jnp.float32)
    return jnp.where(distance <= BW, jnp.exp(-distance / LENGTH_SCALE), jnp.float32(0.0))


def cycle(
    doms, bands, rows, cols, win,
    ens, anc, depth, pos, val, out,
    hb, hw, uw, vw, dw, posb, valb, field, spread, done, relay, chosen, lineage,
    band_send, band_recv, anc_send, anc_recv, s1_send, s1_recv, s2_send, s2_recv, own_sem, load_sem,
):
    me = lax.axis_index("dom")
    band = lax.axis_index("band")
    chunk = cols // doms
    blocks = cols // LANES
    wide = rows + 2 * MARGIN
    body = pl.ds(LANES, cols)

    own = pl.ds(MARGIN, rows)
    loads = [
        pltpu.make_async_copy(src, dst, load_sem.at[i])
        for i, (src, dst) in enumerate(
            [
                (ens.at[0, 0], hb.at[pl.ds(rows, rows)]),
                (ens.at[0, 1], uw.at[own, body]),
                (ens.at[0, 2], vw.at[own, body]),
                (depth, dw.at[own, body]),
            ]
        )
    ]
    for load in loads:
        load.start()

    barrier = pltpu.get_barrier_semaphore()
    for k in range(1, doms):
        pl.semaphore_signal(barrier, inc=1, device_id={"dom": lax.rem(me + k, doms)})

    has_up = band > 0
    has_down = band < bands - 1

    @pl.when(has_up)
    def _():
        pl.semaphore_signal(barrier, inc=1, device_id={"band": band - 1})

    @pl.when(has_down)
    def _():
        pl.semaphore_signal(barrier, inc=1, device_id={"band": band + 1})

    neighbours = jnp.minimum(band, 1) + jnp.minimum(bands - 1 - band, 1)
    pl.semaphore_wait(barrier, doms - 1 + neighbours)

    def band_copies(up, first=0, last=6):
        edge = pl.ds(0, MARGIN) if up else pl.ds(rows - MARGIN, MARGIN)
        halo = pl.ds(MARGIN + rows, MARGIN) if up else pl.ds(0, MARGIN)
        slot = 2 if up else 0
        way = 0 if up else 1
        target = {"band": band - 1} if up else {"band": band + 1}
        pairs = [
            (pos, posb.at[slot]),
            (val, valb.at[slot]),
            (ens.at[0, 0], hb.at[pl.ds(slot * rows, rows)]),
            (ens.at[0, 1, edge], uw.at[halo, body]),
            (ens.at[0, 2, edge], vw.at[halo, body]),
            (depth.at[edge], dw.at[halo, body]),
        ]
        return [
            pltpu.make_async_remote_copy(
                src_ref=src, dst_ref=dst,
                send_sem=band_send.at[way, i], recv_sem=band_recv.at[way, i],
                device_id=target,
            )
            for i, (src, dst) in list(enumerate(pairs))[first:last]
        ]

    @pl.when(has_up)
    def _():
        for copy in band_copies(True):
            copy.start()

    @pl.when(has_down)
    def _():
        for copy in band_copies(False):
            copy.start()

    def anc_copy(k):
        return pltpu.make_async_remote_copy(
            src_ref=anc, dst_ref=lineage.at[me],
            send_sem=anc_send.at[k], recv_sem=anc_recv.at[k],
            device_id={"dom": lax.rem(me + k, doms)},
        )

    for k in range(1, doms):
        anc_copy(k).start()
    lineage[me] = anc[...]

    field[0] = jnp.zeros((3 * rows, LANES), jnp.float32)
    field[blocks + 1] = jnp.zeros((3 * rows, LANES), jnp.float32)

    def place(slot, where_ref, value_ref):
        where, value = where_ref[...], value_ref[...]
        count = where.shape[1]
        group = where >> 7
        lane = where & (LANES - 1)
        high = value.astype(jnp.bfloat16).astype(jnp.float32)
        low = value - high
        hit = lax.broadcasted_iota(jnp.int32, (LANES, count), 0) == lane
        right = jnp.concatenate(
            [
                jnp.where(hit, high, 0.0).astype(jnp.bfloat16),
                jnp.where(hit, low, 0.0).astype(jnp.bfloat16),
                jnp.where(hit, 1.0, 0.0).astype(jnp.bfloat16),
            ],
            axis=0,
        )
        per = 8
        for first in range(0, blocks, per):
            index = lax.broadcasted_iota(jnp.int32, (per * rows, count), 0) + first * rows
            left = jnp.where(index == group, 1.0, 0.0).astype(jnp.bfloat16)
            placed = lax.dot_general(
                left, right, (((1,), (1,)), ((), ())), preferred_element_type=jnp.float32
            )
            for j in range(per):
                part = placed[j * rows : (j + 1) * rows]
                height = hb[slot * rows : (slot + 1) * rows, (first + j) * LANES : (first + j + 1) * LANES]
                field[first + j + 1, slot * rows : (slot + 1) * rows, :] = (
                    part[:, :LANES] + part[:, LANES : 2 * LANES] - part[:, 2 * LANES :] * height
                )

    loads[0].wait()
    place(1, pos, val)

    def blank(slot):
        field[:, slot * rows : (slot + 1) * rows, :] = jnp.zeros(
            (blocks + 2, rows, LANES), jnp.float32
        )
        halo = pl.ds(0, MARGIN) if slot == 0 else pl.ds(MARGIN + rows, MARGIN)
        hb[slot * rows : (slot + 1) * rows] = jnp.zeros((rows, cols), jnp.float32)
        for ref in (uw, vw, dw):
            ref[halo, body] = jnp.zeros((MARGIN, cols), jnp.float32)

    @pl.when(has_up)
    def _():
        for copy in band_copies(False, 0, 3):
            copy.wait_recv()
        place(0, posb.at[0], valb.at[0])

    @pl.when(jnp.logical_not(has_up))
    def _():
        blank(0)

    @pl.when(has_down)
    def _():
        for copy in band_copies(True, 0, 3):
            copy.wait_recv()
        place(2, posb.at[2], valb.at[2])

    @pl.when(jnp.logical_not(has_down))
    def _():
        blank(2)

    apart = lax.broadcasted_iota(jnp.int32, (LANES, LANES), 1) - lax.broadcasted_iota(
        jnp.int32, (LANES, LANES), 0
    )
    mats = [weight(apart + LANES), weight(apart), weight(apart - LANES)]
    global_row = band * rows - MARGIN + lax.broadcasted_iota(jnp.int32, (wide, 1), 0)
    inside = (global_row >= 0) & (global_row < bands * rows)
    per = 8
    for first in range(0, blocks, per):
        total = None
        for i in range(3):
            part = field[first + i : first + i + per].reshape(per * 3 * rows, LANES)
            term = jnp.dot(
                part, mats[i], precision=lax.Precision.HIGHEST, preferred_element_type=jnp.float32
            )
            total = term if total is None else total + term
        spread[first : first + per] = total.reshape(per, 3 * rows, LANES)
    base = rows - MARGIN
    for j in range(blocks):
        increment = None
        for offset in range(2 * BW + 1):
            factor = math.exp(-abs(offset - BW) / LENGTH_SCALE)
            first = base - BW + offset
            term = factor * spread[j, first : first + wide, :]
            increment = term if increment is None else increment + term
        columns = pl.ds(j * LANES, LANES)
        hw[:, (j + 1) * LANES : (j + 2) * LANES] = jnp.where(
            inside, hb[base : base + wide, columns] + NUDGE_GAIN * increment, 0.0
        )

    @pl.when(has_up)
    def _():
        for copy in band_copies(False, 3, 6):
            copy.wait_recv()

    @pl.when(has_down)
    def _():
        for copy in band_copies(True, 3, 6):
            copy.wait_recv()

    for load in loads[1:]:
        load.wait()

    for ref in (hw, uw, vw, dw):
        ref[:, 0:LANES] = ref[:, cols : cols + LANES]
        ref[:, cols + LANES : cols + 2 * LANES] = ref[:, LANES : 2 * LANES]

    turning = 0.1 + 0.4 * ((global_row.astype(jnp.float32) + 0.5) / (bands * rows))
    turn = TIME_STEP * turning
    span = win + 2 * LANES
    windows = cols // win
    each = win // chunk

    def after(x, axis):
        return pltpu.roll(x, x.shape[axis] - 1, axis)

    def before(x, axis):
        return pltpu.roll(x, 1, axis)

    def s1_copy(k, target):
        return pltpu.make_async_remote_copy(
            src_ref=done.at[:, :, pl.ds(pl.multiple_of(target * chunk, LANES), chunk)],
            dst_ref=relay.at[me],
            send_sem=s1_send.at[k], recv_sem=s1_recv.at[k],
            device_id={"dom": target},
        )

    def window(step, carry):
        w = lax.rem(step + me, windows)
        at = pl.ds(pl.multiple_of(w * win, LANES), span)
        h, u, v, d = hw[:, at], uw[:, at], vw[:, at], dw[:, at]
        half = 0.5 * TIME_STEP
        for _ in range(STEPS):
            east, north = d * u, d * v
            diff = (after(east, 1) - before(east, 1)) + (after(north, 0) - before(north, 0))
            h = jnp.where(inside, h - half * diff, 0.0)
            new_u = u + (turn * v - half * (after(h, 1) - before(h, 1)))
            new_v = v - (turn * u + half * (after(h, 0) - before(h, 0)))
            u = jnp.where(inside, new_u, 0.0)
            v = jnp.where(inside, new_v, 0.0)
        target_cols = pl.ds(pl.multiple_of(w * win, LANES), win)
        for i, x in enumerate((h, u, v)):
            done[i, :, target_cols] = x[MARGIN : MARGIN + rows, LANES : LANES + win]
        for i in range(each):
            target = w * each + i

            @pl.when(target != me)
            def _():
                s1_copy(lax.rem(target - me + doms, doms), target).start()

        return carry

    lax.fori_loop(0, windows, window, 0)
    relay[me] = done[:, :, pl.ds(pl.multiple_of(me * chunk, LANES), chunk)]

    for k in range(1, doms):
        anc_copy(k).wait_recv()
        s1_copy(k, lax.rem(me + k, doms)).wait_recv()

    def s2_copy(k):
        target = lax.rem(me + k, doms)
        return pltpu.make_async_remote_copy(
            src_ref=chosen.at[target],
            dst_ref=out.at[0, :, :, pl.ds(pl.multiple_of(me * chunk, LANES), chunk)],
            send_sem=s2_send.at[k], recv_sem=s2_recv.at[k],
            device_id={"dom": target},
        )

    def pick(child):
        parent = lineage[child][0:1, 0:1]
        for i in range(3):
            best = relay[0, i]
            for p in range(1, doms):
                best = jnp.where(parent == p, relay[p, i], best)
            chosen[child, i] = best

    def send(step, carry):
        k = doms // 2 + ((step + 1) // 2) * (1 - 2 * (step % 2))
        pick(lax.rem(me + k, doms))
        s2_copy(k).start()
        return carry

    lax.fori_loop(0, doms - 1, send, 0)
    pick(me)
    own_copy = pltpu.make_async_copy(
        chosen.at[me],
        out.at[0, :, :, pl.ds(pl.multiple_of(me * chunk, LANES), chunk)],
        own_sem,
    )
    own_copy.start()

    @pl.when(has_up)
    def _():
        for copy in band_copies(True):
            copy.wait_send()

    @pl.when(has_down)
    def _():
        for copy in band_copies(False):
            copy.wait_send()

    for k in range(1, doms):
        anc_copy(k).wait_send()
        s1_copy(k, lax.rem(me + k, doms)).wait_send()
    own_copy.wait()
    for k in range(1, doms):
        s2_copy(k).wait()


def on_device(doms, bands, ensemble, ancestors, sea_depth, obs_rows, obs_cols, obs_values):
    _, fields, rows, cols = ensemble.shape
    count = obs_rows.shape[0]
    local_rows = obs_rows - lax.axis_index("band") * rows
    pos = (((obs_cols >> 7) * rows + local_rows) * LANES + (obs_cols & (LANES - 1)))[None, :]
    anc = jnp.broadcast_to(ancestors[:, None], (8, LANES))
    chunk = cols // doms
    blocks = cols // LANES
    win = 1024
    wide = rows + 2 * MARGIN
    f32 = jnp.float32
    dma = pltpu.SemaphoreType.DMA
    vmem = pl.BlockSpec(memory_space=pltpu.VMEM)
    hbm = pl.BlockSpec(memory_space=pltpu.HBM)
    return pl.pallas_call(
        functools.partial(cycle, doms, bands, rows, cols, win),
        out_shape=jax.ShapeDtypeStruct(ensemble.shape, f32),
        in_specs=[hbm, vmem, hbm, vmem, vmem],
        out_specs=pl.BlockSpec(memory_space=pl.ANY),
        scratch_shapes=[
            pltpu.VMEM((3 * rows, cols), f32),
            pltpu.VMEM((wide, cols + 2 * LANES), f32),
            pltpu.VMEM((wide, cols + 2 * LANES), f32),
            pltpu.VMEM((wide, cols + 2 * LANES), f32),
            pltpu.VMEM((wide, cols + 2 * LANES), f32),
            pltpu.VMEM((3, 1, count), jnp.int32),
            pltpu.VMEM((3, 1, count), f32),
            pltpu.VMEM((blocks + 2, 3 * rows, LANES), f32),
            pltpu.VMEM((blocks, 3 * rows, LANES), f32),
            pltpu.VMEM((fields, rows, cols), f32),
            pltpu.VMEM((doms, fields, rows, chunk), f32),
            pltpu.VMEM((doms, fields, rows, chunk), f32),
            pltpu.VMEM((doms, 8, LANES), jnp.int32),
            dma((2, 6)),
            dma((2, 6)),
            dma((doms,)),
            dma((doms,)),
            dma((doms,)),
            dma((doms,)),
            dma((doms,)),
            dma((doms,)),
            dma,
            dma((4,)),
        ],
        compiler_params=pltpu.CompilerParams(
            collective_id=0, has_side_effects=True, vmem_limit_bytes=127 * 512 * 1024
        ),
        name="cycle",
    )(ensemble, anc, sea_depth, pos, obs_values[None, :])


def solution(mesh):
    placed = (
        P("dom", None, "band", None),
        P("dom"),
        P("band", None),
        P("band"),
        P("band"),
        P("band"),
    )
    return jax.shard_map(
        functools.partial(on_device, mesh.shape["dom"], mesh.shape["band"]),
        mesh=mesh,
        in_specs=placed,
        out_specs=P("dom", None, "band", None),
        check_vma=False,
    )
```

```python
import functools
import math

import jax
import jax.numpy as jnp
from jax import lax
from jax.experimental import pallas as pl
from jax.experimental.pallas import tpu as pltpu
from jax.sharding import PartitionSpec as P

STEPS = 4
BW = 8
TIME_STEP = 0.8
NUDGE_GAIN = 0.5
LENGTH_SCALE = 3.0
LANES = 128
MARGIN = 2 * STEPS


def weight(offset):
    distance = jnp.abs(offset).astype(jnp.float32)
    return jnp.where(distance <= BW, jnp.exp(-distance / LENGTH_SCALE), jnp.float32(0.0))


def cycle(
    doms, bands, rows, cols, win,
    ens, anc, depth, pos, val, out,
    hb, hw, uw, vw, dw, posb, valb, field, spread, done, relay, chosen, lineage,
    band_send, band_recv, anc_send, anc_recv, s1_send, s1_recv, s2_send, s2_recv, own_sem, load_sem,
):
    me = lax.axis_index("dom")
    band = lax.axis_index("band")
    chunk = cols // doms
    blocks = cols // LANES
    wide = rows + 2 * MARGIN
    body = pl.ds(LANES, cols)

    own = pl.ds(MARGIN, rows)
    loads = [
        pltpu.make_async_copy(src, dst, load_sem.at[i])
        for i, (src, dst) in enumerate(
            [
                (ens.at[0, 0], hb.at[pl.ds(rows, rows)]),
                (ens.at[0, 1], uw.at[own, body]),
                (ens.at[0, 2], vw.at[own, body]),
                (depth, dw.at[own, body]),
            ]
        )
    ]
    for load in loads:
        load.start()

    barrier = pltpu.get_barrier_semaphore()
    for k in range(1, doms):
        pl.semaphore_signal(barrier, inc=1, device_id={"dom": lax.rem(me + k, doms)})

    has_up = band > 0
    has_down = band < bands - 1

    @pl.when(has_up)
    def _():
        pl.semaphore_signal(barrier, inc=1, device_id={"band": band - 1})

    @pl.when(has_down)
    def _():
        pl.semaphore_signal(barrier, inc=1, device_id={"band": band + 1})

    field[0] = jnp.zeros((3 * rows, LANES), jnp.float32)
    field[blocks + 1] = jnp.zeros((3 * rows, LANES), jnp.float32)

    def place(slot, where_ref, value_ref):
        where, value = where_ref[...], value_ref[...]
        count = where.shape[1]
        group = where >> 7
        lane = where & (LANES - 1)
        high = value.astype(jnp.bfloat16).astype(jnp.float32)
        low = value - high
        hit = lax.broadcasted_iota(jnp.int32, (LANES, count), 0) == lane
        right = jnp.concatenate(
            [
                jnp.where(hit, high, 0.0).astype(jnp.bfloat16),
                jnp.where(hit, low, 0.0).astype(jnp.bfloat16),
                jnp.where(hit, 1.0, 0.0).astype(jnp.bfloat16),
            ],
            axis=0,
        )
        per = 8
        for first in range(0, blocks, per):
            index = lax.broadcasted_iota(jnp.int32, (per * rows, count), 0) + first * rows
            left = jnp.where(index == group, 1.0, 0.0).astype(jnp.bfloat16)
            placed = lax.dot_general(
                left, right, (((1,), (1,)), ((), ())), preferred_element_type=jnp.float32
            )
            for j in range(per):
                part = placed[j * rows : (j + 1) * rows]
                height = hb[slot * rows : (slot + 1) * rows, (first + j) * LANES : (first + j + 1) * LANES]
                field[first + j + 1, slot * rows : (slot + 1) * rows, :] = (
                    part[:, :LANES] + part[:, LANES : 2 * LANES] - part[:, 2 * LANES :] * height
                )

    loads[0].wait()
    place(1, pos, val)

    neighbours = jnp.minimum(band, 1) + jnp.minimum(bands - 1 - band, 1)
    pl.semaphore_wait(barrier, doms - 1 + neighbours)

    def band_copies(up, first=0, last=6):
        edge = pl.ds(0, MARGIN) if up else pl.ds(rows - MARGIN, MARGIN)
        halo = pl.ds(MARGIN + rows, MARGIN) if up else pl.ds(0, MARGIN)
        slot = 2 if up else 0
        way = 0 if up else 1
        target = {"band": band - 1} if up else {"band": band + 1}
        pairs = [
            (pos, posb.at[slot]),
            (val, valb.at[slot]),
            (ens.at[0, 0], hb.at[pl.ds(slot * rows, rows)]),
            (ens.at[0, 1, edge], uw.at[halo, body]),
            (ens.at[0, 2, edge], vw.at[halo, body]),
            (depth.at[edge], dw.at[halo, body]),
        ]
        return [
            pltpu.make_async_remote_copy(
                src_ref=src, dst_ref=dst,
                send_sem=band_send.at[way, i], recv_sem=band_recv.at[way, i],
                device_id=target,
            )
            for i, (src, dst) in list(enumerate(pairs))[first:last]
        ]

    @pl.when(has_up)
    def _():
        for copy in band_copies(True):
            copy.start()

    @pl.when(has_down)
    def _():
        for copy in band_copies(False):
            copy.start()

    def anc_copy(k):
        return pltpu.make_async_remote_copy(
            src_ref=anc, dst_ref=lineage.at[me],
            send_sem=anc_send.at[k], recv_sem=anc_recv.at[k],
            device_id={"dom": lax.rem(me + k, doms)},
        )

    for k in range(1, doms):
        anc_copy(k).start()
    lineage[me] = anc[...]

    def blank(slot):
        field[:, slot * rows : (slot + 1) * rows, :] = jnp.zeros(
            (blocks + 2, rows, LANES), jnp.float32
        )
        halo = pl.ds(0, MARGIN) if slot == 0 else pl.ds(MARGIN + rows, MARGIN)
        hb[slot * rows : (slot + 1) * rows] = jnp.zeros((rows, cols), jnp.float32)
        for ref in (uw, vw, dw):
            ref[halo, body] = jnp.zeros((MARGIN, cols), jnp.float32)

    @pl.when(has_up)
    def _():
        for copy in band_copies(False, 0, 3):
            copy.wait_recv()
        place(0, posb.at[0], valb.at[0])

    @pl.when(jnp.logical_not(has_up))
    def _():
        blank(0)

    @pl.when(has_down)
    def _():
        for copy in band_copies(True, 0, 3):
            copy.wait_recv()
        place(2, posb.at[2], valb.at[2])

    @pl.when(jnp.logical_not(has_down))
    def _():
        blank(2)

    apart = lax.broadcasted_iota(jnp.int32, (LANES, LANES), 1) - lax.broadcasted_iota(
        jnp.int32, (LANES, LANES), 0
    )

    def halves(x):
        high = x.astype(jnp.bfloat16)
        return high, (x - high.astype(jnp.float32)).astype(jnp.bfloat16)

    mats = [halves(weight(apart + shift)) for shift in (LANES, 0, -LANES)]
    global_row = band * rows - MARGIN + lax.broadcasted_iota(jnp.int32, (wide, 1), 0)
    inside = (global_row >= 0) & (global_row < bands * rows)
    per = 8
    for first in range(0, blocks, per):
        total = None
        for i in range(3):
            part = field[first + i : first + i + per].reshape(per * 3 * rows, LANES)
            part_high, part_low = halves(part)
            for x, y in ((part_high, mats[i][0]), (part_low, mats[i][0]), (part_high, mats[i][1])):
                term = jnp.dot(x, y, preferred_element_type=jnp.float32)
                total = term if total is None else total + term
        spread[first : first + per] = total.reshape(per, 3 * rows, LANES)
    base = rows - MARGIN
    for j in range(blocks):
        increment = None
        for offset in range(2 * BW + 1):
            factor = math.exp(-abs(offset - BW) / LENGTH_SCALE)
            first = base - BW + offset
            term = factor * spread[j, first : first + wide, :]
            increment = term if increment is None else increment + term
        columns = pl.ds(j * LANES, LANES)
        hw[:, (j + 1) * LANES : (j + 2) * LANES] = jnp.where(
            inside, hb[base : base + wide, columns] + NUDGE_GAIN * increment, 0.0
        )

    @pl.when(has_up)
    def _():
        for copy in band_copies(False, 3, 6):
            copy.wait_recv()

    @pl.when(has_down)
    def _():
        for copy in band_copies(True, 3, 6):
            copy.wait_recv()

    for load in loads[1:]:
        load.wait()

    for ref in (hw, uw, vw, dw):
        ref[:, 0:LANES] = ref[:, cols : cols + LANES]
        ref[:, cols + LANES : cols + 2 * LANES] = ref[:, LANES : 2 * LANES]

    turning = 0.1 + 0.4 * ((global_row.astype(jnp.float32) + 0.5) / (bands * rows))
    turn = TIME_STEP * turning
    span = win + 2 * LANES
    windows = cols // win
    each = win // chunk

    def after(x, axis):
        return pltpu.roll(x, x.shape[axis] - 1, axis)

    def before(x, axis):
        return pltpu.roll(x, 1, axis)

    def s1_copy(k, target):
        return pltpu.make_async_remote_copy(
            src_ref=done.at[:, :, pl.ds(pl.multiple_of(target * chunk, LANES), chunk)],
            dst_ref=relay.at[me],
            send_sem=s1_send.at[k], recv_sem=s1_recv.at[k],
            device_id={"dom": target},
        )

    def window(step, carry):
        w = lax.rem(step + me, windows)
        at = pl.ds(pl.multiple_of(w * win, LANES), span)
        h, u, v, d = hw[:, at], uw[:, at], vw[:, at], dw[:, at]
        half = 0.5 * TIME_STEP
        for _ in range(STEPS):
            east, north = d * u, d * v
            diff = (after(east, 1) - before(east, 1)) + (after(north, 0) - before(north, 0))
            h = jnp.where(inside, h - half * diff, 0.0)
            new_u = u + (turn * v - half * (after(h, 1) - before(h, 1)))
            new_v = v - (turn * u + half * (after(h, 0) - before(h, 0)))
            u = jnp.where(inside, new_u, 0.0)
            v = jnp.where(inside, new_v, 0.0)
        target_cols = pl.ds(pl.multiple_of(w * win, LANES), win)
        for i, x in enumerate((h, u, v)):
            done[i, :, target_cols] = x[MARGIN : MARGIN + rows, LANES : LANES + win]
        for i in range(each):
            target = w * each + i

            @pl.when(target != me)
            def _():
                s1_copy(lax.rem(target - me + doms, doms), target).start()

        return carry

    lax.fori_loop(0, windows, window, 0)
    relay[me] = done[:, :, pl.ds(pl.multiple_of(me * chunk, LANES), chunk)]

    for k in range(1, doms):
        anc_copy(k).wait_recv()
        s1_copy(k, lax.rem(me + k, doms)).wait_recv()

    def s2_copy(k):
        target = lax.rem(me + k, doms)
        return pltpu.make_async_remote_copy(
            src_ref=chosen.at[target],
            dst_ref=out.at[0, :, :, pl.ds(pl.multiple_of(me * chunk, LANES), chunk)],
            send_sem=s2_send.at[k], recv_sem=s2_recv.at[k],
            device_id={"dom": target},
        )

    def pick(child):
        parent = lineage[child][0:1, 0:1]
        for i in range(3):
            best = relay[0, i]
            for p in range(1, doms):
                best = jnp.where(parent == p, relay[p, i], best)
            chosen[child, i] = best

    def send(k, carry):
        pick(lax.rem(me + k, doms))
        s2_copy(k).start()
        return carry

    lax.fori_loop(1, doms, send, 0)
    pick(me)
    own_copy = pltpu.make_async_copy(
        chosen.at[me],
        out.at[0, :, :, pl.ds(pl.multiple_of(me * chunk, LANES), chunk)],
        own_sem,
    )
    own_copy.start()

    @pl.when(has_up)
    def _():
        for copy in band_copies(True):
            copy.wait_send()

    @pl.when(has_down)
    def _():
        for copy in band_copies(False):
            copy.wait_send()

    for k in range(1, doms):
        anc_copy(k).wait_send()
        s1_copy(k, lax.rem(me + k, doms)).wait_send()
    own_copy.wait()
    for k in range(1, doms):
        s2_copy(k).wait()


def on_device(doms, bands, ensemble, ancestors, sea_depth, obs_rows, obs_cols, obs_values):
    _, fields, rows, cols = ensemble.shape
    count = obs_rows.shape[0]
    local_rows = obs_rows - lax.axis_index("band") * rows
    pos = (((obs_cols >> 7) * rows + local_rows) * LANES + (obs_cols & (LANES - 1)))[None, :]
    anc = jnp.broadcast_to(ancestors[:, None], (8, LANES))
    chunk = cols // doms
    blocks = cols // LANES
    win = 1024
    wide = rows + 2 * MARGIN
    f32 = jnp.float32
    dma = pltpu.SemaphoreType.DMA
    vmem = pl.BlockSpec(memory_space=pltpu.VMEM)
    hbm = pl.BlockSpec(memory_space=pltpu.HBM)
    return pl.pallas_call(
        functools.partial(cycle, doms, bands, rows, cols, win),
        out_shape=jax.ShapeDtypeStruct(ensemble.shape, f32),
        in_specs=[hbm, vmem, hbm, vmem, vmem],
        out_specs=pl.BlockSpec(memory_space=pl.ANY),
        scratch_shapes=[
            pltpu.VMEM((3 * rows, cols), f32),
            pltpu.VMEM((wide, cols + 2 * LANES), f32),
            pltpu.VMEM((wide, cols + 2 * LANES), f32),
            pltpu.VMEM((wide, cols + 2 * LANES), f32),
            pltpu.VMEM((wide, cols + 2 * LANES), f32),
            pltpu.VMEM((3, 1, count), jnp.int32),
            pltpu.VMEM((3, 1, count), f32),
            pltpu.VMEM((blocks + 2, 3 * rows, LANES), f32),
            pltpu.VMEM((blocks, 3 * rows, LANES), f32),
            pltpu.VMEM((fields, rows, cols), f32),
            pltpu.VMEM((doms, fields, rows, chunk), f32),
            pltpu.VMEM((doms, fields, rows, chunk), f32),
            pltpu.VMEM((doms, 8, LANES), jnp.int32),
            dma((2, 6)),
            dma((2, 6)),
            dma((doms,)),
            dma((doms,)),
            dma((doms,)),
            dma((doms,)),
            dma((doms,)),
            dma((doms,)),
            dma,
            dma((4,)),
        ],
        compiler_params=pltpu.CompilerParams(
            collective_id=0, has_side_effects=True, vmem_limit_bytes=127 * 512 * 1024
        ),
        name="cycle",
    )(ensemble, anc, sea_depth, pos, obs_values[None, :])


def solution(mesh):
    placed = (
        P("dom", None, "band", None),
        P("dom"),
        P("band", None),
        P("band"),
        P("band"),
        P("band"),
    )
    return jax.shard_map(
        functools.partial(on_device, mesh.shape["dom"], mesh.shape["band"]),
        mesh=mesh,
        in_specs=placed,
        out_specs=P("dom", None, "band", None),
        check_vma=False,
    )
```

```python
import functools
import math

import jax
import jax.numpy as jnp
from jax import lax
from jax.experimental import pallas as pl
from jax.experimental.pallas import tpu as pltpu
from jax.sharding import PartitionSpec as P

STEPS = 4
BW = 8
TIME_STEP = 0.8
NUDGE_GAIN = 0.5
LENGTH_SCALE = 3.0
LANES = 128
MARGIN = 2 * STEPS


def weight(offset):
    distance = jnp.abs(offset).astype(jnp.float32)
    return jnp.where(distance <= BW, jnp.exp(-distance / LENGTH_SCALE), jnp.float32(0.0))


def cycle(
    doms, bands, rows, cols, win,
    ens, anc, depth, pos, val, out,
    hb, hw, uw, vw, dw, posb, valb, field, spread, done, relay, chosen, lineage,
    band_send, band_recv, anc_send, anc_recv, s1_send, s1_recv, s2_send, s2_recv, own_sem,
):
    me = lax.axis_index("dom")
    band = lax.axis_index("band")
    chunk = cols // doms
    blocks = cols // LANES
    wide = rows + 2 * MARGIN
    body = pl.ds(LANES, cols)

    barrier = pltpu.get_barrier_semaphore()
    for k in range(1, doms):
        pl.semaphore_signal(barrier, inc=1, device_id={"dom": lax.rem(me + k, doms)})

    has_up = band > 0
    has_down = band < bands - 1

    @pl.when(has_up)
    def _():
        pl.semaphore_signal(barrier, inc=1, device_id={"band": band - 1})

    @pl.when(has_down)
    def _():
        pl.semaphore_signal(barrier, inc=1, device_id={"band": band + 1})

    neighbours = jnp.minimum(band, 1) + jnp.minimum(bands - 1 - band, 1)
    pl.semaphore_wait(barrier, doms - 1 + neighbours)

    def band_copies(up, first=0, last=6):
        edge = pl.ds(0, MARGIN) if up else pl.ds(rows - MARGIN, MARGIN)
        halo = pl.ds(MARGIN + rows, MARGIN) if up else pl.ds(0, MARGIN)
        slot = 2 if up else 0
        way = 0 if up else 1
        target = {"band": band - 1} if up else {"band": band + 1}
        pairs = [
            (pos, posb.at[slot]),
            (val, valb.at[slot]),
            (ens.at[0, 0], hb.at[pl.ds(slot * rows, rows)]),
            (ens.at[0, 1, edge], uw.at[halo, body]),
            (ens.at[0, 2, edge], vw.at[halo, body]),
            (depth.at[edge], dw.at[halo, body]),
        ]
        return [
            pltpu.make_async_remote_copy(
                src_ref=src, dst_ref=dst,
                send_sem=band_send.at[way, i], recv_sem=band_recv.at[way, i],
                device_id=target,
            )
            for i, (src, dst) in list(enumerate(pairs))[first:last]
        ]

    @pl.when(has_up)
    def _():
        for copy in band_copies(True):
            copy.start()

    @pl.when(has_down)
    def _():
        for copy in band_copies(False):
            copy.start()

    def anc_copy(k):
        return pltpu.make_async_remote_copy(
            src_ref=anc, dst_ref=lineage.at[me],
            send_sem=anc_send.at[k], recv_sem=anc_recv.at[k],
            device_id={"dom": lax.rem(me + k, doms)},
        )

    for k in range(1, doms):
        anc_copy(k).start()
    lineage[me] = anc[...]

    own = pl.ds(MARGIN, rows)
    hb[rows : 2 * rows] = ens[0, 0]
    uw[own, body] = ens[0, 1]
    vw[own, body] = ens[0, 2]
    dw[own, body] = depth[...]
    field[0] = jnp.zeros((3 * rows, LANES), jnp.float32)
    field[blocks + 1] = jnp.zeros((3 * rows, LANES), jnp.float32)

    def place(slot, where_ref, value_ref):
        where, value = where_ref[...], value_ref[...]
        count = where.shape[1]
        group = where >> 7
        lane = where & (LANES - 1)
        high = value.astype(jnp.bfloat16).astype(jnp.float32)
        low = value - high
        hit = lax.broadcasted_iota(jnp.int32, (LANES, count), 0) == lane
        right = jnp.concatenate(
            [
                jnp.where(hit, high, 0.0).astype(jnp.bfloat16),
                jnp.where(hit, low, 0.0).astype(jnp.bfloat16),
                jnp.where(hit, 1.0, 0.0).astype(jnp.bfloat16),
            ],
            axis=0,
        )
        per = 8
        for first in range(0, blocks, per):
            index = lax.broadcasted_iota(jnp.int32, (per * rows, count), 0) + first * rows
            left = jnp.where(index == group, 1.0, 0.0).astype(jnp.bfloat16)
            placed = lax.dot_general(
                left, right, (((1,), (1,)), ((), ())), preferred_element_type=jnp.float32
            )
            for j in range(per):
                part = placed[j * rows : (j + 1) * rows]
                height = hb[slot * rows : (slot + 1) * rows, (first + j) * LANES : (first + j + 1) * LANES]
                field[first + j + 1, slot * rows : (slot + 1) * rows, :] = (
                    part[:, :LANES] + part[:, LANES : 2 * LANES] - part[:, 2 * LANES :] * height
                )

    place(1, pos, val)

    def blank(slot):
        field[:, slot * rows : (slot + 1) * rows, :] = jnp.zeros(
            (blocks + 2, rows, LANES), jnp.float32
        )
        halo = pl.ds(0, MARGIN) if slot == 0 else pl.ds(MARGIN + rows, MARGIN)
        hb[slot * rows : (slot + 1) * rows] = jnp.zeros((rows, cols), jnp.float32)
        for ref in (uw, vw, dw):
            ref[halo, body] = jnp.zeros((MARGIN, cols), jnp.float32)

    @pl.when(has_up)
    def _():
        for copy in band_copies(False, 0, 3):
            copy.wait_recv()
        place(0, posb.at[0], valb.at[0])

    @pl.when(jnp.logical_not(has_up))
    def _():
        blank(0)

    @pl.when(has_down)
    def _():
        for copy in band_copies(True, 0, 3):
            copy.wait_recv()
        place(2, posb.at[2], valb.at[2])

    @pl.when(jnp.logical_not(has_down))
    def _():
        blank(2)

    apart = lax.broadcasted_iota(jnp.int32, (LANES, LANES), 1) - lax.broadcasted_iota(
        jnp.int32, (LANES, LANES), 0
    )
    mats = [weight(apart + LANES), weight(apart), weight(apart - LANES)]
    global_row = band * rows - MARGIN + lax.broadcasted_iota(jnp.int32, (wide, 1), 0)
    inside = (global_row >= 0) & (global_row < bands * rows)
    per = 8
    for first in range(0, blocks, per):
        total = None
        for i in range(3):
            part = field[first + i : first + i + per].reshape(per * 3 * rows, LANES)
            term = jnp.dot(
                part, mats[i], precision=lax.Precision.HIGHEST, preferred_element_type=jnp.float32
            )
            total = term if total is None else total + term
        spread[first : first + per] = total.reshape(per, 3 * rows, LANES)
    base = rows - MARGIN
    for j in range(blocks):
        increment = None
        for offset in range(2 * BW + 1):
            factor = math.exp(-abs(offset - BW) / LENGTH_SCALE)
            first = base - BW + offset
            term = factor * spread[j, first : first + wide, :]
            increment = term if increment is None else increment + term
        columns = pl.ds(j * LANES, LANES)
        hw[:, (j + 1) * LANES : (j + 2) * LANES] = jnp.where(
            inside, hb[base : base + wide, columns] + NUDGE_GAIN * increment, 0.0
        )

    @pl.when(has_up)
    def _():
        for copy in band_copies(False, 3, 6):
            copy.wait_recv()

    @pl.when(has_down)
    def _():
        for copy in band_copies(True, 3, 6):
            copy.wait_recv()

    for ref in (hw, uw, vw, dw):
        ref[:, 0:LANES] = ref[:, cols : cols + LANES]
        ref[:, cols + LANES : cols + 2 * LANES] = ref[:, LANES : 2 * LANES]

    turning = 0.1 + 0.4 * ((global_row.astype(jnp.float32) + 0.5) / (bands * rows))
    turn = TIME_STEP * turning
    span = win + 2 * LANES
    windows = cols // win
    each = win // chunk

    def after(x, axis):
        return pltpu.roll(x, x.shape[axis] - 1, axis)

    def before(x, axis):
        return pltpu.roll(x, 1, axis)

    def s1_copy(k, target):
        return pltpu.make_async_remote_copy(
            src_ref=done.at[:, :, pl.ds(pl.multiple_of(target * chunk, LANES), chunk)],
            dst_ref=relay.at[me],
            send_sem=s1_send.at[k], recv_sem=s1_recv.at[k],
            device_id={"dom": target},
        )

    def window(step, carry):
        w = lax.rem(step + me, windows)
        at = pl.ds(pl.multiple_of(w * win, LANES), span)
        h, u, v, d = hw[:, at], uw[:, at], vw[:, at], dw[:, at]
        half = 0.5 * TIME_STEP
        for _ in range(STEPS):
            east, north = d * u, d * v
            diff = (after(east, 1) - before(east, 1)) + (after(north, 0) - before(north, 0))
            h = jnp.where(inside, h - half * diff, 0.0)
            new_u = u + (turn * v - half * (after(h, 1) - before(h, 1)))
            new_v = v - (turn * u + half * (after(h, 0) - before(h, 0)))
            u = jnp.where(inside, new_u, 0.0)
            v = jnp.where(inside, new_v, 0.0)
        target_cols = pl.ds(pl.multiple_of(w * win, LANES), win)
        for i, x in enumerate((h, u, v)):
            done[i, :, target_cols] = x[MARGIN : MARGIN + rows, LANES : LANES + win]
        for i in range(each):
            target = w * each + i

            @pl.when(target != me)
            def _():
                s1_copy(lax.rem(target - me + doms, doms), target).start()

        return carry

    lax.fori_loop(0, windows, window, 0)
    relay[me] = done[:, :, pl.ds(pl.multiple_of(me * chunk, LANES), chunk)]

    for k in range(1, doms):
        anc_copy(k).wait_recv()
        s1_copy(k, lax.rem(me + k, doms)).wait_recv()

    def s2_copy(k):
        target = lax.rem(me + k, doms)
        return pltpu.make_async_remote_copy(
            src_ref=chosen.at[target],
            dst_ref=out.at[0, :, :, pl.ds(pl.multiple_of(me * chunk, LANES), chunk)],
            send_sem=s2_send.at[k], recv_sem=s2_recv.at[k],
            device_id={"dom": target},
        )

    def pick(child):
        parent = lineage[child][0:1, 0:1]
        for i in range(3):
            best = relay[0, i]
            for p in range(1, doms):
                best = jnp.where(parent == p, relay[p, i], best)
            chosen[child, i] = best

    def send(k, carry):
        pick(lax.rem(me + k, doms))
        s2_copy(k).start()
        return carry

    lax.fori_loop(1, doms, send, 0)
    pick(me)
    own_copy = pltpu.make_async_copy(
        chosen.at[me],
        out.at[0, :, :, pl.ds(pl.multiple_of(me * chunk, LANES), chunk)],
        own_sem,
    )
    own_copy.start()

    @pl.when(has_up)
    def _():
        for copy in band_copies(True):
            copy.wait_send()

    @pl.when(has_down)
    def _():
        for copy in band_copies(False):
            copy.wait_send()

    for k in range(1, doms):
        anc_copy(k).wait_send()
        s1_copy(k, lax.rem(me + k, doms)).wait_send()
    own_copy.wait()
    for k in range(1, doms):
        s2_copy(k).wait()


def on_device(doms, bands, ensemble, ancestors, sea_depth, obs_rows, obs_cols, obs_values):
    _, fields, rows, cols = ensemble.shape
    count = obs_rows.shape[0]
    local_rows = obs_rows - lax.axis_index("band") * rows
    pos = (((obs_cols >> 7) * rows + local_rows) * LANES + (obs_cols & (LANES - 1)))[None, :]
    anc = jnp.broadcast_to(ancestors[:, None], (8, LANES))
    chunk = cols // doms
    blocks = cols // LANES
    win = 512
    wide = rows + 2 * MARGIN
    f32 = jnp.float32
    dma = pltpu.SemaphoreType.DMA
    vmem = pl.BlockSpec(memory_space=pltpu.VMEM)
    return pl.pallas_call(
        functools.partial(cycle, doms, bands, rows, cols, win),
        out_shape=jax.ShapeDtypeStruct(ensemble.shape, f32),
        in_specs=[vmem] * 5,
        out_specs=pl.BlockSpec(memory_space=pl.ANY),
        scratch_shapes=[
            pltpu.VMEM((3 * rows, cols), f32),
            pltpu.VMEM((wide, cols + 2 * LANES), f32),
            pltpu.VMEM((wide, cols + 2 * LANES), f32),
            pltpu.VMEM((wide, cols + 2 * LANES), f32),
            pltpu.VMEM((wide, cols + 2 * LANES), f32),
            pltpu.VMEM((3, 1, count), jnp.int32),
            pltpu.VMEM((3, 1, count), f32),
            pltpu.VMEM((blocks + 2, 3 * rows, LANES), f32),
            pltpu.VMEM((blocks, 3 * rows, LANES), f32),
            pltpu.VMEM((fields, rows, cols), f32),
            pltpu.VMEM((doms, fields, rows, chunk), f32),
            pltpu.VMEM((doms, fields, rows, chunk), f32),
            pltpu.VMEM((doms, 8, LANES), jnp.int32),
            dma((2, 6)),
            dma((2, 6)),
            dma((doms,)),
            dma((doms,)),
            dma((doms,)),
            dma((doms,)),
            dma((doms,)),
            dma((doms,)),
            dma,
        ],
        compiler_params=pltpu.CompilerParams(
            collective_id=0, has_side_effects=True, vmem_limit_bytes=48 * 1024 * 1024
        ),
        name="cycle",
    )(ensemble, anc, sea_depth, pos, obs_values[None, :])


def solution(mesh):
    placed = (
        P("dom", None, "band", None),
        P("dom"),
        P("band", None),
        P("band"),
        P("band"),
        P("band"),
    )
    return jax.shard_map(
        functools.partial(on_device, mesh.shape["dom"], mesh.shape["band"]),
        mesh=mesh,
        in_specs=placed,
        out_specs=P("dom", None, "band", None),
        check_vma=False,
    )
```
